512 devices in a mesh: vocab: 32 (over x, y), width: 16 (over z, core).
Axes of the slice: x: 4, y: 8, z: 8, core: 2. Of those that a mesh axis runs over, the one named last changes fastest.
Arguments:
- hidden: bfloat16 [448, 4608], P(None, 'width'), may hold values from -30 to 30
- head_weight: bfloat16 [65536, 4608], P('vocab', 'width'), may hold values from -0.09375 to 0.09375
- targets: int32 [448], replicated, may hold values from 0 to 65535
- lse_rest: float32 [448], replicated, may hold values from 18 to 23
- cotangent: float32 [448], replicated, may hold values from 0.3 to 3
Outputs:
- grad_hidden: bfloat16 [448, 4608], P(None, 'width')
- grad_weight: bfloat16 [65536, 4608], P('vocab', 'width')
- token_loss: float32 [448], P('width')
The draws below stay inside these ranges and needn't reach their ends.
All inputs are finite; a program needn't handle non-finite values.
Results may differ from the reference program's by a relative error of at most 0.0051.
Values may be sent and summed in bfloat16 or wider, within the bound.
No kernel may reach another device: no remote copies, remote signals or barrier semaphores. Data moves between devices by JAX's collectives and lax.ppermute only.
A program may use at most 64 MiB of HBM per device.

```python
import math
import jax
import jax.numpy as jnp

D = 4608
VOCAB = 65536
TOK = 448


def touch_ends(entries, stream_key, smallest, high):
    extent = entries.shape
    spot = [jax.random.randint(jax.random.fold_in(stream_key, axis), (), 0, extent[axis]) for axis in range(len(extent))]
    entries = entries.at[tuple(spot)].set(smallest)
    longest = extent.index(max(extent))
    spot[longest] = (spot[longest] + 1) % extent[longest]
    return entries.at[tuple(spot)].set(high)


def level_of(rng, dims, pieces, smallest, largest):
    def one(axis_at, blocks):
        heights = jax.random.uniform(jax.random.fold_in(jax.random.fold_in(rng, 6), axis_at), (blocks,), jnp.float32, smallest / len(pieces), largest / len(pieces))
        return jnp.repeat(jnp.exp(heights), dims[axis_at] // blocks).reshape((-1,) + (1,) * (len(dims) - axis_at - 1))

    level = one(*pieces[0])
    for cut in pieces[1:]:
        level = level * one(*cut)
    return level


def gaussian(stream_key, dims, scale, bound, pieces=(), kind=jnp.bfloat16):
    factor_of = level_of(stream_key, dims, pieces, -0.22, 0.18) if pieces else 1.0
    values = jax.random.normal(stream_key, dims, jnp.float32) * scale * factor_of
    return jnp.minimum(jnp.maximum(values, -bound), bound).astype(kind)


def setup_inputs(seed: int = 0) -> dict:
    key_list = jax.random.split(jax.random.key(seed), 6)
    hidden = gaussian(key_list[0], (TOK, D), 5.0, 30.0, ((1, 16),))
    head_weight = gaussian(key_list[1], (VOCAB, D), D ** -0.5, 0.09375, ((0, 32), (1, 16)))
    targets = touch_ends(jax.random.randint(key_list[2], (TOK,), 0, VOCAB), jax.random.fold_in(key_list[2], 1), 0, VOCAB - 1).astype(jnp.int32)
    lse_rest = jnp.clip(jax.random.uniform(key_list[3], (TOK,), jnp.float32, 18.0, 23.0), 18.0, 23.0)
    cotangent = jnp.clip(jnp.exp(jax.random.uniform(key_list[4], (TOK,), jnp.float32, math.log(0.3), math.log(3.0))), 0.3, 3.0)
    return dict(hidden=hidden, head_weight=head_weight, targets=targets, lse_rest=lse_rest, cotangent=cotangent)


soft_cap = 30.0
zloss_weight = 0.002


def reference(hidden, head_weight, targets, lse_rest, cotangent):
    logits = jnp.dot(hidden, head_weight.T, preferred_element_type=jnp.float32)
    capped = soft_cap * jnp.tanh(logits / soft_cap)
    slab_lse = jnp.log(jnp.sum(jnp.exp(capped), axis=1))
    onehot = (jnp.arange(VOCAB, dtype=jnp.int32)[None, :] == targets[:, None]).astype(jnp.float32)
    picked = jnp.sum(capped * onehot, axis=1)
    lse = jnp.logaddexp(slab_lse, lse_rest)
    token_loss = lse - picked + zloss_weight * lse * lse
    scale = 1.0 + 2.0 * zloss_weight * lse
    dcap = cotangent[:, None] * (jnp.exp(capped - lse[:, None]) * scale[:, None] - onehot)
    ratio = capped / soft_cap
    dlogit = (dcap * (1.0 - ratio * ratio)).astype(jnp.bfloat16)
    grad_hidden = jnp.dot(dlogit, head_weight, preferred_element_type=jnp.float32).astype(jnp.bfloat16)
    grad_weight = jnp.dot(dlogit.T, hidden, preferred_element_type=jnp.float32).astype(jnp.bfloat16)
    return grad_hidden, grad_weight, token_loss
```

```python
import jax
import jax.numpy as jnp
from jax import lax
from jax.experimental import pallas as pl
from jax.experimental.pallas import tpu as pltpu
from jax.sharding import Mesh, PartitionSpec as P

soft_cap = 30.0
zloss_weight = 0.002
wire = jnp.bfloat16
tokens = 448
lanes = 128


def params(**kw):
    return pltpu.CompilerParams(vmem_limit_bytes=32 * 1024 * 1024, **kw)


def half_logits(which, hidden_t, weight_t, received=None):
    depth = hidden_t.shape[0]

    def kernel(which_ref, h_ref, w_ref, *refs):
        out_ref, turned = refs[-2:]

        @pl.when(pl.program_id(0) == 0)
        def _():
            turned[...] = jnp.transpose(h_ref[...])

        part = jnp.dot(turned[...], w_ref[...], preferred_element_type=jnp.float32)
        for i in range(2):
            block = part[:, i * lanes : (i + 1) * lanes]
            if received is not None:
                block = block + refs[0][i].astype(jnp.float32)
            out_ref[i] = block.astype(wire)

    blocks = pl.BlockSpec((2, tokens, lanes), lambda i, c: (i, 0, 0))
    in_specs = [
        pl.BlockSpec((depth, tokens), lambda i, c: (0, 0)),
        pl.BlockSpec((depth, 2 * lanes), lambda i, c: (0, c[0] * 4 + i)),
    ]
    operands = [which, hidden_t, weight_t]
    if received is not None:
        in_specs.append(blocks)
        operands.append(received)
    return pl.pallas_call(
        kernel,
        grid_spec=pltpu.PrefetchScalarGridSpec(
            num_scalar_prefetch=1,
            grid=(4,),
            in_specs=in_specs,
            out_specs=blocks,
            scratch_shapes=[pltpu.VMEM((tokens, depth), jnp.bfloat16)],
        ),
        out_shape=jax.ShapeDtypeStruct((8, tokens, lanes), wire),
        compiler_params=params(),
    )(*operands)


def rows_of(vector):
    out = [vector[:, r * lanes : (r + 1) * lanes] for r in range(3)]
    tail = vector[:, 3 * lanes :]
    return out + [jnp.concatenate([tail, jnp.zeros((1, 4 * lanes - tokens), vector.dtype)], axis=1)]


def soften(first_column, parts, target_column):
    def kernel(first_ref, parts_ref, target_ref, out_ref):
        logits = parts_ref[0].astype(jnp.float32)
        for i in range(1, 8):
            logits = logits + parts_ref[i].astype(jnp.float32)
        ratio = jnp.tanh(logits * (1.0 / soft_cap))
        capped = soft_cap * ratio
        power = jnp.exp(capped - soft_cap)
        soft = (power * (1.0 - ratio * ratio)).astype(jnp.bfloat16)
        columns = lax.broadcasted_iota(jnp.int32, (tokens, lanes), 1) + first_ref[0]
        hit = jnp.where(columns == target_ref[...], capped, 0.0)
        ones = jnp.ones((8, lanes), jnp.float32)

        def total(block):
            return lax.dot_general(
                ones,
                block,
                (((1,), (1,)), ((), ())),
                precision=lax.Precision.HIGHEST,
                preferred_element_type=jnp.float32,
            )[0:1]

        row = lax.broadcasted_iota(jnp.int32, (16, lanes), 0)
        tile = jnp.zeros((16, lanes), jnp.float32)
        for k, sums in enumerate((total(power), total(hit))):
            for r, piece in enumerate(rows_of(sums)):
                high = piece.astype(jnp.bfloat16).astype(jnp.float32)
                tile = jnp.where(row == 8 * k + r, high, tile)
                tile = jnp.where(row == 8 * k + 4 + r, piece - high, tile)
        tile = tile.astype(jnp.bfloat16)
        for i in range(8):
            out_ref[i, :tokens] = soft
            out_ref[i, tokens:] = tile

    return pl.pallas_call(
        kernel,
        in_specs=[
            pl.BlockSpec(memory_space=pltpu.SMEM),
            pl.BlockSpec(memory_space=pltpu.VMEM),
            pl.BlockSpec(memory_space=pltpu.VMEM),
        ],
        out_specs=pl.BlockSpec(memory_space=pltpu.VMEM),
        out_shape=jax.ShapeDtypeStruct((8, tokens + 16, lanes), jnp.bfloat16),
        compiler_params=params(),
    )(first_column, parts, target_column)


def spread_sums(own, other):
    def kernel(own_ref, other_ref, out_ref):
        both = jnp.zeros((16, lanes), jnp.float32)
        for i in range(8):
            both = both + (own_ref[i].astype(jnp.float32) + other_ref[i].astype(jnp.float32))
        tile = jnp.concatenate([both[0:4] + both[4:8], both[8:12] + both[12:16]], axis=0)
        for i in range(32):
            out_ref[i] = tile

    spec = pl.BlockSpec((8, 16, lanes), lambda i: (0, tokens // 16, 0))
    return pl.pallas_call(
        kernel,
        grid=(1,),
        in_specs=[spec, spec],
        out_specs=pl.BlockSpec((32, 8, lanes), lambda i: (0, 0, 0)),
        out_shape=jax.ShapeDtypeStruct((32, 8, lanes), jnp.float32),
        compiler_params=params(),
    )(own, other)


def gradients(index, sums, rest_row, cot_row, target_column, own, other, hidden_t, weight_t):
    depth = hidden_t.shape[0]

    def kernel(
        index_ref, sums_ref, rest_ref, cot_ref, target_ref, own_ref, other_ref, h_ref, w_ref,
        gh_ref, gw_ref, loss_ref, total, factors,
    ):
        step = pl.program_id(0)

        @pl.when(step == 0)
        def _():
            tile = sums_ref[0]
            for i in range(1, 32):
                tile = tile + sums_ref[i]
            row = lax.broadcasted_iota(jnp.int32, (8, lanes), 0)
            rest = jnp.zeros((8, lanes), jnp.float32)
            cot = jnp.zeros((8, lanes), jnp.float32)
            for r, (a, b) in enumerate(zip(rows_of(rest_ref[...]), rows_of(cot_ref[...]))):
                rest = jnp.where(row == r, a, rest)
                cot = jnp.where((row == r) | (row == r + 4), b, cot)
            slab = jnp.log(tile) + soft_cap
            larger, smaller = jnp.maximum(slab, rest), jnp.minimum(slab, rest)
            lse = larger + jnp.log(1.0 + jnp.exp(smaller - larger))
            picked = jnp.concatenate([tile[4:8], tile[0:4]], axis=0)
            loss_ref[...] = lse - picked + zloss_weight * lse * lse
            scale = cot * (1.0 + 2.0 * zloss_weight * lse) * jnp.exp(soft_cap - lse)
            ratio = tile * (1.0 / soft_cap)
            hit = cot * (1.0 - ratio * ratio)
            turned = jnp.transpose(jnp.where(row < 4, scale, hit))
            for r in range(4):
                size = min(lanes, tokens - r * lanes)
                factors[r * lanes : r * lanes + size, 0:1] = turned[:size, r : r + 1]
                factors[r * lanes : r * lanes + size, 1:2] = turned[:size, r + 4 : r + 5]
            total[...] = jnp.zeros_like(total)

        half = jnp.where(step < 4, index_ref[0], 1 - index_ref[0])
        first = index_ref[1] + half * 8 * lanes + lax.rem(step, 4) * 2 * lanes
        scale, hit = factors[:, 0:1], factors[:, 1:2]
        blocks = []
        for i in range(2):
            block = jnp.where(step < 4, own_ref[i], other_ref[i]).astype(jnp.float32)
            columns = lax.broadcasted_iota(jnp.int32, (tokens, lanes), 1) + (first + i * lanes)
            onehot = jnp.where(columns == target_ref[...], hit, 0.0)
            blocks.append((block * scale - onehot).astype(jnp.bfloat16))
        dlogit = jnp.concatenate(blocks, axis=1)
        total[...] += lax.dot_general(
            dlogit, w_ref[...], (((1,), (1,)), ((), ())), preferred_element_type=jnp.float32
        )
        gw_ref[...] = jnp.dot(
            h_ref[...], dlogit, preferred_element_type=jnp.float32
        ).astype(jnp.bfloat16)

        @pl.when(step == 7)
        def _():
            gh_ref[:tokens] = total[...].astype(wire)
            gh_ref[tokens:] = jnp.zeros((512 - tokens, depth), wire)

    def whole(shape):
        return pl.BlockSpec(shape, lambda j, c: (0,) * len(shape))

    def vocab_block(j, c):
        half = jnp.where(j < 4, c[0], 1 - c[0])
        return (0, half * 4 + lax.rem(j, 4))

    return pl.pallas_call(
        kernel,
        grid_spec=pltpu.PrefetchScalarGridSpec(
            num_scalar_prefetch=1,
            grid=(8,),
            in_specs=[
                whole((32, 8, lanes)),
                whole((1, tokens)),
                whole((1, tokens)),
                whole((tokens, 1)),
                pl.BlockSpec((2, tokens, lanes), lambda j, c: (jnp.minimum(j, 3), 0, 0)),
                pl.BlockSpec((2, tokens, lanes), lambda j, c: (jnp.maximum(j - 4, 0), 0, 0)),
                whole((depth, tokens)),
                pl.BlockSpec((depth, 2 * lanes), vocab_block),
            ],
            out_specs=[
                whole((512, depth)),
                pl.BlockSpec((depth, 2 * lanes), vocab_block),
                whole((8, lanes)),
            ],
            scratch_shapes=[
                pltpu.VMEM((tokens, depth), jnp.float32),
                pltpu.VMEM((tokens, lanes), jnp.float32),
            ],
        ),
        out_shape=[
            jax.ShapeDtypeStruct((512, depth), wire),
            jax.ShapeDtypeStruct((depth, 2048), jnp.bfloat16),
            jax.ShapeDtypeStruct((8, lanes), jnp.float32),
        ],
        compiler_params=params(),
    )(index, sums, rest_row, cot_row, target_column, own, other, hidden_t, weight_t)


def add_and_spread(parts):
    def kernel(parts_ref, out_ref):
        total = parts_ref[0].astype(jnp.float32)
        for i in range(1, 32):
            total = total + parts_ref[i].astype(jnp.float32)
        total = total.astype(jnp.bfloat16)
        for i in range(32):
            out_ref[i] = total

    return pl.pallas_call(
        kernel,
        in_specs=[pl.BlockSpec(memory_space=pltpu.VMEM)],
        out_specs=pl.BlockSpec(memory_space=pltpu.VMEM),
        out_shape=jax.ShapeDtypeStruct(parts.shape, jnp.bfloat16),
        compiler_params=params(),
    )(parts)


def per_device(hidden, head_weight, targets, lse_rest, cotangent):
    x, y, z, core = (lax.axis_index(a) for a in ("x", "y", "z", "core"))
    swap = [(0, 1), (1, 0)]
    vocab_first = (x * 8 + y) * 2048
    first = vocab_first + core * 1024 + z * lanes
    index = jnp.stack([core, vocab_first]).astype(jnp.int32)
    target_column = targets.reshape(tokens, 1)
    hidden_t, weight_t = hidden.T, head_weight.T

    sent = half_logits((1 - core).reshape(1).astype(jnp.int32), hidden_t, weight_t)
    received = lax.ppermute(sent, "core", swap)
    mine = half_logits(core.reshape(1).astype(jnp.int32), hidden_t, weight_t, received)
    parts = lax.all_to_all(mine, "z", 0, 0, tiled=True)
    soft = soften(first.reshape(1).astype(jnp.int32), parts, target_column)
    own = lax.all_to_all(soft, "z", 0, 0, tiled=True)
    other = lax.ppermute(own, "core", swap)
    sums = lax.all_to_all(spread_sums(own, other), ("x", "y"), 0, 0, tiled=True)
    grad_part, grad_weight, losses = gradients(
        index,
        sums,
        lse_rest.reshape(1, tokens),
        cotangent.reshape(1, tokens),
        target_column,
        own,
        other,
        hidden_t,
        weight_t,
    )
    depth = hidden.shape[1]
    shares = lax.all_to_all(grad_part.reshape(32, 16, depth), ("x", "y"), 0, 0, tiled=True)
    whole = lax.all_to_all(add_and_spread(shares), ("x", "y"), 0, 0, tiled=True)
    grad_hidden = whole.reshape(512, depth)[:tokens]
    share = tokens // 16
    token_loss = lax.dynamic_slice_in_dim(losses.reshape(-1), (z * 2 + core) * share, share, 0)
    return (grad_hidden, grad_weight.T, token_loss)


def solution(mesh):
    mesh = Mesh(mesh.devices.reshape(4, 8, 8, 2), ("x", "y", "z", "core"))
    vocab, width = ("x", "y"), ("z", "core")
    return jax.shard_map(
        per_device,
        mesh=mesh,
        in_specs=(P(None, width), P(vocab, width), P(), P(), P()),
        out_specs=(P(None, width), P(vocab, width), P(width)),
        check_vma=False,
    )
```

```python
import jax
import jax.numpy as jnp
from jax import lax
from jax.experimental import pallas as pl
from jax.experimental.pallas import tpu as pltpu
from jax.sharding import Mesh, PartitionSpec as P

soft_cap = 30.0
zloss_weight = 0.002
tokens = 448
lanes = 128
chunk = 16
shards = 32
filled = tokens // chunk
padded = 384
bf16, f32 = jnp.bfloat16, jnp.float32
vmem = pl.BlockSpec(memory_space=pltpu.VMEM)
smem = pl.BlockSpec(memory_space=pltpu.SMEM)


def call(kernel, out_shape, in_specs, scratch=()):
    several = isinstance(out_shape, (list, tuple))
    return pl.pallas_call(
        kernel,
        in_specs=in_specs,
        out_specs=[vmem] * len(out_shape) if several else vmem,
        out_shape=out_shape,
        scratch_shapes=scratch,
        compiler_params=pltpu.CompilerParams(vmem_limit_bytes=32 * 1024 * 1024),
    )


def iota(shape, axis):
    return lax.broadcasted_iota(jnp.int32, shape, axis)


def sent_logits(core, hidden_t, weight_t):
    def kernel(core_ref, h_ref, w_ref, out_ref):
        h = jnp.transpose(h_ref[...])
        for i in range(4):
            at = pl.multiple_of((1 - core_ref[0]) * 1024 + i * 256, 256)
            part = jnp.dot(h, w_ref[:, pl.ds(at, 256)], preferred_element_type=f32)
            out_ref[2 * i] = part[:, :lanes].astype(bf16)
            out_ref[2 * i + 1] = part[:, lanes:].astype(bf16)

    out = jax.ShapeDtypeStruct((8, tokens, lanes), bf16)
    return call(kernel, out, [smem, vmem, vmem])(core, hidden_t, weight_t)


def kept_logits(core, hidden_t, weight_t, received):
    def kernel(core_ref, h_ref, w_ref, got_ref, out_ref):
        h = jnp.transpose(h_ref[...])
        for i in range(4):
            at = pl.multiple_of(core_ref[0] * 1024 + i * 256, 256)
            part = jnp.dot(h, w_ref[:, pl.ds(at, 256)], preferred_element_type=f32)
            for k in range(2):
                block = part[:, k * lanes : (k + 1) * lanes] + got_ref[2 * i + k].astype(f32)
                out_ref[2 * i + k] = block.astype(bf16)

    out = jax.ShapeDtypeStruct((8, tokens, lanes), bf16)
    return call(kernel, out, [smem, vmem, vmem, vmem])(core, hidden_t, weight_t, received)


def high_low(tile):
    high = tile.astype(bf16).astype(f32)
    return [high, tile - high]


def soften(first_column, parts, target_column):
    def kernel(first_ref, parts_ref, target_ref, out_ref):
        logits = parts_ref[0].astype(f32)
        for i in range(1, 8):
            logits = logits + parts_ref[i].astype(f32)
        ratio = jnp.tanh(logits * (1.0 / soft_cap))
        capped = soft_cap * ratio
        power = jnp.exp(capped - soft_cap)
        soft = (power * (1.0 - ratio * ratio)).astype(bf16)
        hit = jnp.where(iota((tokens, lanes), 1) + first_ref[0] == target_ref[...], capped, 0.0)

        def total(block):
            return lax.dot_general(
                jnp.ones((8, lanes), f32),
                block,
                (((1,), (1,)), ((), ())),
                precision=lax.Precision.HIGHEST,
                preferred_element_type=f32,
            )[0:1]

        row = iota((16, lanes), 0)
        tile = jnp.zeros((16, lanes), f32)
        for k, sums in enumerate((total(power), total(hit))):
            pieces = [sums[:, r * lanes : (r + 1) * lanes] for r in range(3)]
            tail = jnp.zeros((1, 4 * lanes - tokens), f32)
            pieces.append(jnp.concatenate([sums[:, 3 * lanes :], tail], axis=1))
            for r, piece in enumerate(pieces):
                high, low = high_low(piece)
                tile = jnp.where(row == 8 * k + r, high, tile)
                tile = jnp.where(row == 8 * k + 4 + r, low, tile)
        tile = tile.astype(bf16)
        for i in range(8):
            out_ref[i, :tokens] = soft
            out_ref[i, tokens:] = tile

    out = jax.ShapeDtypeStruct((8, tokens + chunk, lanes), bf16)
    return call(kernel, out, [smem, vmem, vmem])(first_column, parts, target_column)


def columns_of(rows):
    turned = jnp.transpose(rows)
    out = []
    for at in range(0, rows.shape[0], 4):
        pieces = [turned[: min(lanes, tokens - r * lanes), at + r : at + r + 1] for r in range(4)]
        out.append(jnp.broadcast_to(jnp.concatenate(pieces, axis=0), (tokens, lanes)))
    return out


def unscaled(index, own, other, target_column, cot_rows, weight_t):
    depth = weight_t.shape[0]

    def kernel(index_ref, own_ref, other_ref, target_ref, cot_ref, w_ref, out_ref, hits, total):
        sums = jnp.zeros((chunk, lanes), f32)
        for i in range(8):
            sums = sums + (own_ref[i, tokens:].astype(f32) + other_ref[i, tokens:].astype(f32))
        powers, picked = sums[0:4] + sums[4:8], sums[8:12] + sums[12:16]
        ratio = picked * (1.0 / soft_cap)
        scale = cot_ref[...] * (1.0 - ratio * ratio)
        rows = high_low(powers) + high_low(picked) + [scale] * 4
        columns = columns_of(jnp.concatenate(rows, axis=0))
        hits[...] = columns[4]
        for j in range(8):
            which = index_ref[0] if j < 4 else 1 - index_ref[0]
            at = pl.multiple_of(which * 1024 + (j % 4) * 256, 256)
            blocks = []
            for k in range(2):
                place = 2 * (j % 4) + k
                soft = own_ref[place, :tokens] if j < 4 else other_ref[place, :tokens]
                column = iota((tokens, lanes), 1) + (index_ref[1] + at + k * lanes)
                hit = jnp.where(column == target_ref[...], hits[...], 0.0).astype(bf16)
                blocks.append(jnp.concatenate([soft, hit], axis=0))
            product = lax.dot_general(
                jnp.concatenate(blocks, axis=1),
                w_ref[:, pl.ds(at, 256)],
                (((1,), (1,)), ((), ())),
                preferred_element_type=f32,
            )
            if j == 0:
                total[...] = product
            else:
                total[...] += product
        lane = iota((tokens, lanes), 1)
        last = jnp.concatenate([total[:tokens, 256:], jnp.zeros((tokens, padded - depth), f32)], axis=1)
        for k in range(4):
            last = jnp.where(lane == depth - 256 + k, columns[k], last)
        out_ref[:filled, :chunk, :256] = total[:tokens, :256].astype(bf16).reshape(filled, chunk, 256)
        out_ref[:filled, :chunk, 256:] = last.astype(bf16).reshape(filled, chunk, lanes)
        out_ref[:filled, chunk:, :depth] = total[tokens:].astype(bf16).reshape(filled, chunk, depth)
        out_ref[:filled, chunk:, depth:] = jnp.zeros((filled, chunk, padded - depth), bf16)
        out_ref[filled:] = jnp.zeros((shards - filled, 2 * chunk, padded), bf16)

    return call(
        kernel,
        [
            jax.ShapeDtypeStruct((shards, 2 * chunk, padded), bf16),
            jax.ShapeDtypeStruct((tokens, lanes), f32),
        ],
        [smem, vmem, vmem, vmem, vmem, vmem],
        [pltpu.VMEM((2 * tokens, depth), f32)],
    )(index, own, other, target_column, cot_rows, weight_t)


def reduce_chunk(shard, parts, rest_and_cot, depth):
    def kernel(shard_ref, parts_ref, small_ref, out_ref):
        total = parts_ref[0].astype(f32)
        for i in range(1, shards):
            total = total + parts_ref[i].astype(f32)
        mine = small_ref[pl.ds(pl.multiple_of(shard_ref[0] * chunk, chunk), chunk)]
        rest, cot = mine[:, 0:1], mine[:, 1:2]
        power = total[:chunk, depth : depth + 1] + total[:chunk, depth + 1 : depth + 2]
        picked = total[:chunk, depth + 2 : depth + 3] + total[:chunk, depth + 3 : depth + 4]
        slab = jnp.log(power) + soft_cap
        larger, smaller = jnp.maximum(slab, rest), jnp.minimum(slab, rest)
        lse = larger + jnp.log(1.0 + jnp.exp(smaller - larger))
        loss = lse - picked + zloss_weight * lse * lse
        scale = cot * (1.0 + 2.0 * zloss_weight * lse) * jnp.exp(soft_cap - lse)
        out = total[:chunk] * scale - total[chunk:]
        lane = iota((chunk, padded), 1)
        for k, column in enumerate(high_low(scale) + high_low(loss)):
            out = jnp.where(lane == depth + k, column, out)
        out = out.astype(bf16)
        for i in range(shards):
            out_ref[i] = out

    out = jax.ShapeDtypeStruct((shards, chunk, padded), bf16)
    return call(kernel, out, [smem, vmem, vmem])(shard, parts, rest_and_cot)


def finish(index, reduced, own, other, hits, target_column, hidden_t):
    depth = hidden_t.shape[0]
    share = tokens // 16

    def kernel(
        index_ref, reduced_ref, own_ref, other_ref, hits_ref, target_ref, h_ref,
        gh_ref, gw_ref, loss_ref, scales, losses,
    ):
        last = reduced_ref[:filled, :, 256:].reshape(tokens, lanes).astype(f32)
        at = depth - 256
        scales[...] = jnp.broadcast_to(last[:, at : at + 1] + last[:, at + 1 : at + 2], (tokens, lanes))
        losses[:tokens] = jnp.broadcast_to(last[:, at + 2 : at + 3] + last[:, at + 3 : at + 4], (tokens, lanes))
        loss_ref[...] = jnp.transpose(losses[pl.ds(index_ref[2] * share, 32)])[0:1, :share]
        summed = reduced_ref[:filled].reshape(tokens, padded).astype(f32)
        gh_ref[...] = jnp.transpose(summed)[:depth].astype(bf16)
        for j in range(8):
            which = index_ref[0] if j < 4 else 1 - index_ref[0]
            at = pl.multiple_of(which * 1024 + (j % 4) * 256, 256)
            blocks = []
            for k in range(2):
                place = 2 * (j % 4) + k
                block = own_ref[place, :tokens] if j < 4 else other_ref[place, :tokens]
                column = iota((tokens, lanes), 1) + (index_ref[1] + at + k * lanes)
                hit = jnp.where(column == target_ref[...], hits_ref[...], 0.0)
                blocks.append((block.astype(f32) * scales[...] - hit).astype(bf16))
            product = jnp.dot(
                h_ref[...], jnp.concatenate(blocks, axis=1), preferred_element_type=f32
            )
            gw_ref[:, pl.ds(at, 256)] = product.astype(bf16)

    return call(
        kernel,
        [
            jax.ShapeDtypeStruct((depth, tokens), bf16),
            jax.ShapeDtypeStruct((depth, 2048), bf16),
            jax.ShapeDtypeStruct((1, share), f32),
        ],
        [smem] + [vmem] * 6,
        [pltpu.VMEM((tokens, lanes), f32), pltpu.VMEM((tokens + 32, lanes), f32)],
    )(index, reduced, own, other, hits, target_column, hidden_t)


def per_device(hidden, head_weight, targets, lse_rest, cotangent):
    x, y, z, core = (lax.axis_index(a).astype(jnp.int32) for a in ("x", "y", "z", "core"))
    swap = [(0, 1), (1, 0)]
    vocab = ("x", "y")
    shard = x * 8 + y
    index = jnp.stack([core, shard * 2048, z * 2 + core])
    first = (shard * 2048 + core * 1024 + z * lanes).reshape(1)
    target_column = targets.reshape(tokens, 1)
    rest_and_cot = jnp.pad(
        jnp.stack([lse_rest, cotangent], axis=1), ((0, shards * chunk - tokens), (0, 0))
    )
    cot_rows = jnp.pad(cotangent, (0, 4 * lanes - tokens)).reshape(4, lanes)
    hidden_t, weight_t = hidden.T, head_weight.T

    sent = sent_logits(index, hidden_t, weight_t)
    received = lax.ppermute(sent, "core", swap)
    mine = kept_logits(index, hidden_t, weight_t, received)
    parts = lax.all_to_all(mine, "z", 0, 0, tiled=True)
    own = lax.all_to_all(soften(first, parts, target_column), "z", 0, 0, tiled=True)
    other = lax.ppermute(own, "core", swap)
    part, hits = unscaled(index, own, other, target_column, cot_rows, weight_t)
    shares = lax.all_to_all(part, vocab, 0, 0, tiled=True)
    spread = reduce_chunk(shard.reshape(1), shares, rest_and_cot, hidden.shape[1])
    reduced = lax.all_to_all(spread, vocab, 0, 0, tiled=True)
    grad_hidden, grad_weight, token_loss = finish(
        index, reduced, own, other, hits, target_column, hidden_t
    )
    return (grad_hidden.T, grad_weight.T, token_loss.reshape(-1))


def solution(mesh):
    mesh = Mesh(mesh.devices.reshape(4, 8, 8, 2), ("x", "y", "z", "core"))
    vocab, width = ("x", "y"), ("z", "core")
    return jax.shard_map(
        per_device,
        mesh=mesh,
        in_specs=(P(None, width), P(vocab, width), P(), P(), P()),
        out_specs=(P(None, width), P(vocab, width), P(width)),
        check_vma=False,
    )
```

```python
import jax
import jax.numpy as jnp
from jax import lax
from jax.experimental import pallas as pl
from jax.experimental.pallas import tpu as pltpu
from jax.sharding import Mesh, PartitionSpec as P

soft_cap = 30.0
zloss_weight = 0.002
tokens = 448
lanes = 128
chunk = 16
shards = 32
filled = tokens // chunk
padded = 384
packed = 640
bf16, f32 = jnp.bfloat16, jnp.float32
vmem = pl.BlockSpec(memory_space=pltpu.VMEM)
smem = pl.BlockSpec(memory_space=pltpu.SMEM)


def call(kernel, out_shape, in_specs, scratch=()):
    several = isinstance(out_shape, (list, tuple))
    return pl.pallas_call(
        kernel,
        in_specs=in_specs,
        out_specs=[vmem] * len(out_shape) if several else vmem,
        out_shape=out_shape,
        scratch_shapes=scratch,
        compiler_params=pltpu.CompilerParams(vmem_limit_bytes=32 * 1024 * 1024),
    )


def iota(shape, axis):
    return lax.broadcasted_iota(jnp.int32, shape, axis)


def rows_of(vector):
    out = [vector[:, r * lanes : (r + 1) * lanes] for r in range(3)]
    tail = jnp.zeros((1, 4 * lanes - tokens), vector.dtype)
    return out + [jnp.concatenate([vector[:, 3 * lanes :], tail], axis=1)]


def columns_of(rows):
    turned = jnp.transpose(rows)
    out = []
    for at in range(0, rows.shape[0], 4):
        pieces = [turned[: min(lanes, tokens - r * lanes), at + r : at + r + 1] for r in range(4)]
        out.append(jnp.broadcast_to(jnp.concatenate(pieces, axis=0), (tokens, lanes)))
    return out


def half_logits(index, hidden_t, weight_t, vectors=()):
    depth = hidden_t.shape[0]
    own = bool(vectors)
    kind = f32 if own else bf16

    def kernel(index_ref, h_ref, w_ref, *refs):
        turned = refs[-1]
        out_ref = refs[3] if own else refs[0]

        @pl.when(pl.program_id(0) == 0)
        def _():
            turned[...] = jnp.transpose(h_ref[...])
            if own:
                target_ref, rest_ref, cot_ref = refs[:3]
                rows = rows_of(target_ref[...].astype(f32)) + rows_of(rest_ref[...]) + rows_of(cot_ref[...])
                tile = jnp.zeros((16, lanes), f32)
                for r, row in enumerate(rows):
                    tile = jnp.where(iota((16, lanes), 0) == r, row, tile)
                target, rest, cot, _ = columns_of(tile)
                refs[4][...] = target
                refs[5][:tokens] = jnp.where(iota((tokens, lanes), 1) == 0, rest, cot)
                refs[5][tokens:] = jnp.zeros((shards * chunk - tokens, lanes), f32)

        part = jnp.dot(turned[...], w_ref[...], preferred_element_type=f32).astype(kind)
        out_ref[0] = part[:, :lanes]
        out_ref[1] = part[:, lanes:]

    def whole(*shape):
        return pl.BlockSpec(shape, lambda i, c: (0,) * len(shape))

    def block(i, c):
        return (0, (c[0] if own else 1 - c[0]) * 4 + i)

    out_specs = [pl.BlockSpec((2, tokens, lanes), lambda i, c: (i, 0, 0))]
    out_shape = [jax.ShapeDtypeStruct((8, tokens, lanes), kind)]
    if own:
        out_specs += [whole(tokens, lanes), whole(shards * chunk, lanes)]
        out_shape += [jax.ShapeDtypeStruct(spec.block_shape, f32) for spec in out_specs[1:]]
    return pl.pallas_call(
        kernel,
        grid_spec=pltpu.PrefetchScalarGridSpec(
            num_scalar_prefetch=1,
            grid=(4,),
            in_specs=[whole(depth, tokens), pl.BlockSpec((depth, 256), block)]
            + [whole(1, tokens)] * len(vectors),
            out_specs=out_specs,
            scratch_shapes=[pltpu.VMEM((tokens, depth), bf16)],
        ),
        out_shape=out_shape,
        compiler_params=pltpu.CompilerParams(vmem_limit_bytes=(32 if own else 60) * 1024 * 1024),
    )(index, hidden_t, weight_t, *vectors)


def add_halves(kept, received):
    def kernel(kept_ref, received_ref, out_ref):
        for i in range(8):
            out_ref[i] = (kept_ref[i] + received_ref[i].astype(f32)).astype(bf16)

    return call(kernel, jax.ShapeDtypeStruct(kept.shape, bf16), [vmem, vmem])(kept, received)


def high_low(tile):
    high = tile.astype(bf16).astype(f32)
    return [high, tile - high]


def soften(index, parts, target):
    def kernel(index_ref, parts_ref, target_ref, out_ref):
        logits = parts_ref[0].astype(f32)
        for i in range(1, 8):
            logits = logits + parts_ref[i].astype(f32)
        ratio = jnp.tanh(logits * (1.0 / soft_cap))
        capped = soft_cap * ratio
        power = jnp.exp(capped - soft_cap)
        soft = (power * (1.0 - ratio * ratio)).astype(bf16)
        first = index_ref[1] + index_ref[0] * 1024 + (index_ref[2] // 2) * lanes
        columns = (iota((tokens, lanes), 1) + first).astype(f32)
        hit = jnp.where(columns == target_ref[...], capped, 0.0)

        def total(block):
            return lax.dot_general(
                jnp.ones((8, lanes), f32),
                block,
                (((1,), (1,)), ((), ())),
                precision=lax.Precision.HIGHEST,
                preferred_element_type=f32,
            )[0:1]

        row = iota((16, lanes), 0)
        tile = jnp.zeros((16, lanes), f32)
        for k, sums in enumerate((total(power), total(hit))):
            for r, piece in enumerate(rows_of(sums)):
                high, low = high_low(piece)
                tile = jnp.where(row == 8 * k + r, high, tile)
                tile = jnp.where(row == 8 * k + 4 + r, low, tile)
        tile = tile.astype(bf16)
        for i in range(8):
            out_ref[i, :tokens] = soft
            out_ref[i, tokens:] = tile

    out = jax.ShapeDtypeStruct((8, tokens + chunk, lanes), bf16)
    return call(kernel, out, [smem, vmem, vmem])(index, parts, target)


def half_grad(index, soft, target, small, weight_t, before=()):
    depth = weight_t.shape[0]
    last = bool(before)

    def kernel(index_ref, soft_ref, target_ref, small_ref, w_ref, *refs):
        sums = jnp.zeros((chunk, lanes), f32)
        for i in range(8):
            sums = sums + soft_ref[i, tokens:].astype(f32)
        if last:
            sums = sums + refs[1][...]
        rows = [sums[0:4] + sums[4:8], sums[8:12] + sums[12:16]]
        power, picked = columns_of(jnp.concatenate(rows, axis=0))
        ratio = picked * (1.0 / soft_cap)
        cot = jnp.broadcast_to(small_ref[:tokens, 1:2], (tokens, lanes))
        hits = cot * (1.0 - ratio * ratio)
        total = refs[-1]
        which = 1 - index_ref[0] if last else index_ref[0]
        for j in range(4):
            at = pl.multiple_of(which * 1024 + j * 256, 256)
            blocks = []
            for k in range(2):
                column = (iota((tokens, lanes), 1) + (index_ref[1] + at + k * lanes)).astype(f32)
                hit = jnp.where(column == target_ref[...], hits, 0.0).astype(bf16)
                blocks.append(jnp.concatenate([soft_ref[2 * j + k, :tokens], hit], axis=0))
            product = lax.dot_general(
                jnp.concatenate(blocks, axis=1),
                w_ref[:, pl.ds(at, 256)],
                (((1,), (1,)), ((), ())),
                preferred_element_type=f32,
            )
            if j:
                total[...] += product
            elif last:
                total[...] = refs[0][...] + product
            else:
                total[...] = product
        if not last:
            refs[1][...] = sums
            return
        out_ref, hits_ref = refs[2:4]
        hits_ref[...] = hits
        first, second = total[:tokens], total[tokens:]
        lane = iota((tokens, lanes), 1)
        end = jnp.concatenate([second[:, 224:], jnp.zeros((tokens, lanes - depth + 224), f32)], axis=1)
        for k, column in enumerate(high_low(power) + high_low(picked)):
            end = jnp.where(lane == depth - 224 + k, column, end)
        middle = jnp.concatenate([first[:, 256:], second[:, :96]], axis=1)
        for t, piece in enumerate((first[:, :lanes], first[:, lanes:256], middle, second[:, 96:224], end)):
            out_ref[:filled, :, t * lanes : (t + 1) * lanes] = piece.astype(bf16).reshape(filled, chunk, lanes)
        out_ref[filled:] = jnp.zeros((shards - filled, chunk, packed), bf16)

    total = (2 * tokens, depth)
    if last:
        out = [
            jax.ShapeDtypeStruct((shards, chunk, packed), bf16),
            jax.ShapeDtypeStruct((tokens, lanes), f32),
        ]
        scratch = [pltpu.VMEM(total, f32)]
    else:
        out = [jax.ShapeDtypeStruct((chunk, lanes), f32), jax.ShapeDtypeStruct(total, f32)]
        out = [out[1], out[0]]
        scratch = []
    inside = kernel if last else lambda *refs: kernel(*refs, refs[5])
    return call(inside, out, [smem] + [vmem] * (4 + len(before)), scratch)(
        index, soft, target, small, weight_t, *before
    )


def reduce_chunk(index, parts, small, depth):
    def kernel(index_ref, parts_ref, small_ref, out_ref):
        total = parts_ref[0].astype(f32)
        for i in range(1, shards):
            total = total + parts_ref[i].astype(f32)
        mine = small_ref[pl.ds(pl.multiple_of(index_ref[3] * chunk, chunk), chunk)]
        rest, cot = mine[:, 0:1], mine[:, 1:2]
        at = 2 * depth
        power = total[:, at : at + 1] + total[:, at + 1 : at + 2]
        picked = total[:, at + 2 : at + 3] + total[:, at + 3 : at + 4]
        slab = jnp.log(power) + soft_cap
        larger, smaller = jnp.maximum(slab, rest), jnp.minimum(slab, rest)
        lse = larger + jnp.log(1.0 + jnp.exp(smaller - larger))
        loss = lse - picked + zloss_weight * lse * lse
        scale = cot * (1.0 + 2.0 * zloss_weight * lse) * jnp.exp(soft_cap - lse)
        out = total[:, :depth] * scale - total[:, depth:at]
        out = jnp.concatenate([out, jnp.zeros((chunk, padded - depth), f32)], axis=1)
        lane = iota((chunk, padded), 1)
        for k, column in enumerate(high_low(scale) + high_low(loss)):
            out = jnp.where(lane == depth + k, column, out)
        out = out.astype(bf16)
        for i in range(shards):
            out_ref[i] = out

    out = jax.ShapeDtypeStruct((shards, chunk, padded), bf16)
    return call(kernel, out, [smem, vmem, vmem])(index, parts, small)


def finish(index, reduced, own, other, hits, target, hidden_t):
    depth = hidden_t.shape[0]
    share = tokens // 16

    def kernel(
        index_ref, reduced_ref, own_ref, other_ref, hits_ref, target_ref, h_ref,
        gh_ref, gw_ref, loss_ref, scales, losses,
    ):
        last = reduced_ref[:filled, :, 256:].reshape(tokens, lanes).astype(f32)
        at = depth - 256
        scales[...] = jnp.broadcast_to(last[:, at : at + 1] + last[:, at + 1 : at + 2], (tokens, lanes))
        losses[:tokens] = jnp.broadcast_to(last[:, at + 2 : at + 3] + last[:, at + 3 : at + 4], (tokens, lanes))
        loss_ref[...] = jnp.transpose(losses[pl.ds(index_ref[2] * share, 32)])[0:1, :share]
        summed = reduced_ref[:filled].reshape(tokens, padded).astype(f32)
        gh_ref[...] = jnp.transpose(summed)[:depth].astype(bf16)
        for j in range(8):
            which = index_ref[0] if j < 4 else 1 - index_ref[0]
            at = pl.multiple_of(which * 1024 + (j % 4) * 256, 256)
            blocks = []
            for k in range(2):
                place = 2 * (j % 4) + k
                block = own_ref[place, :tokens] if j < 4 else other_ref[place, :tokens]
                column = (iota((tokens, lanes), 1) + (index_ref[1] + at + k * lanes)).astype(f32)
                hit = jnp.where(column == target_ref[...], hits_ref[...], 0.0)
                blocks.append((block.astype(f32) * scales[...] - hit).astype(bf16))
            product = jnp.dot(
                h_ref[...], jnp.concatenate(blocks, axis=1), preferred_element_type=f32
            )
            gw_ref[:, pl.ds(at, 256)] = product.astype(bf16)

    return call(
        kernel,
        [
            jax.ShapeDtypeStruct((depth, tokens), bf16),
            jax.ShapeDtypeStruct((depth, 2048), bf16),
            jax.ShapeDtypeStruct((1, share), f32),
        ],
        [smem] + [vmem] * 6,
        [pltpu.VMEM((tokens, lanes), f32), pltpu.VMEM((tokens + 32, lanes), f32)],
    )(index, reduced, own, other, hits, target, hidden_t)


def per_device(hidden, head_weight, targets, lse_rest, cotangent):
    x, y, z, core = (lax.axis_index(a).astype(jnp.int32) for a in ("x", "y", "z", "core"))
    swap = [(0, 1), (1, 0)]
    vocab = ("x", "y")
    shard = x * 8 + y
    index = jnp.stack([core, shard * 2048, z * 2 + core, shard])
    hidden_t, weight_t = hidden.T, head_weight.T
    vectors = [v.reshape(1, tokens) for v in (targets, lse_rest, cotangent)]

    (sent,) = half_logits(index, hidden_t, weight_t)
    received = lax.ppermute(sent, "core", swap)
    kept, target, small = half_logits(index, hidden_t, weight_t, vectors)
    parts = lax.all_to_all(add_halves(kept, received), "z", 0, 0, tiled=True)
    own = lax.all_to_all(soften(index, parts, target), "z", 0, 0, tiled=True)
    other = lax.ppermute(own, "core", swap)
    before = half_grad(index, own, target, small, weight_t)
    part, hits = half_grad(index, other, target, small, weight_t, before)
    shares = lax.all_to_all(part, vocab, 0, 0, tiled=True)
    spread = reduce_chunk(index, shares, small, hidden.shape[1])
    reduced = lax.all_to_all(spread, vocab, 0, 0, tiled=True)
    grad_hidden, grad_weight, token_loss = finish(
        index, reduced, own, other, hits, target, hidden_t
    )
    return (grad_hidden.T, grad_weight.T, token_loss.reshape(-1))


def solution(mesh):
    mesh = Mesh(mesh.devices.reshape(4, 8, 8, 2), ("x", "y", "z", "core"))
    vocab, width = ("x", "y"), ("z", "core")
    return jax.shard_map(
        per_device,
        mesh=mesh,
        in_specs=(P(None, width), P(vocab, width), P(), P(), P()),
        out_specs=(P(None, width), P(vocab, width), P(width)),
        check_vma=False,
    )
```

```python
import jax
import jax.numpy as jnp
from jax import lax
from jax.experimental import pallas as pl
from jax.experimental.pallas import tpu as pltpu
from jax.sharding import Mesh, PartitionSpec as P

soft_cap = 30.0
zloss_weight = 0.002
tokens = 448
lanes = 128
chunk = 16
shards = 32
filled = tokens // chunk
padded = 384
packed = 640
bf16, f32 = jnp.bfloat16, jnp.float32
vmem = pl.BlockSpec(memory_space=pltpu.VMEM)
smem = pl.BlockSpec(memory_space=pltpu.SMEM)
hbm = pl.BlockSpec(memory_space=pltpu.HBM)


def call(kernel, out_shape, in_specs, scratch=()):
    several = isinstance(out_shape, (list, tuple))
    return pl.pallas_call(
        kernel,
        in_specs=in_specs,
        out_specs=[vmem] * len(out_shape) if several else vmem,
        out_shape=out_shape,
        scratch_shapes=scratch,
        compiler_params=pltpu.CompilerParams(vmem_limit_bytes=32 * 1024 * 1024),
    )


def iota(shape, axis):
    return lax.broadcasted_iota(jnp.int32, shape, axis)


def rows_of(vector):
    out = [vector[:, r * lanes : (r + 1) * lanes] for r in range(3)]
    tail = jnp.zeros((1, 4 * lanes - tokens), vector.dtype)
    return out + [jnp.concatenate([vector[:, 3 * lanes :], tail], axis=1)]


def columns_of(rows):
    turned = jnp.transpose(rows)
    out = []
    for at in range(0, rows.shape[0], 4):
        pieces = [turned[: min(lanes, tokens - r * lanes), at + r : at + r + 1] for r in range(4)]
        out.append(jnp.broadcast_to(jnp.concatenate(pieces, axis=0), (tokens, lanes)))
    return out


def sent_logits(index, hidden_t, weight_t):
    depth = hidden_t.shape[0]

    def kernel(index_ref, h_hbm, w_hbm, out_ref, h_ref, w_ref, arrived):
        half = pl.multiple_of((1 - index_ref[0]) * 1024, 1024)
        first = pltpu.make_async_copy(h_hbm, h_ref, arrived.at[0])
        second = pltpu.make_async_copy(w_hbm.at[:, pl.ds(half, 1024)], w_ref, arrived.at[1])
        first.start()
        second.start()
        first.wait()
        h = jnp.transpose(h_ref[...])
        second.wait()
        for i in range(4):
            part = jnp.dot(h, w_ref[:, i * 256 : (i + 1) * 256], preferred_element_type=f32)
            out_ref[2 * i] = part[:, :lanes].astype(bf16)
            out_ref[2 * i + 1] = part[:, lanes:].astype(bf16)

    return pl.pallas_call(
        kernel,
        in_specs=[smem, hbm, hbm],
        out_specs=vmem,
        out_shape=jax.ShapeDtypeStruct((8, tokens, lanes), bf16),
        scratch_shapes=[
            pltpu.VMEM((depth, tokens), bf16),
            pltpu.VMEM((depth, 1024), bf16),
            pltpu.SemaphoreType.DMA((2,)),
        ],
        compiler_params=pltpu.CompilerParams(vmem_limit_bytes=60 * 1024 * 1024),
    )(index, hidden_t, weight_t)


def kept_logits(index, hidden_t, weight_t, vectors):
    def kernel(index_ref, h_ref, w_ref, target_ref, rest_ref, cot_ref, out_ref, wanted_ref, small_ref):
        rows = rows_of(target_ref[...].astype(f32)) + rows_of(rest_ref[...]) + rows_of(cot_ref[...])
        tile = jnp.zeros((16, lanes), f32)
        for r, row in enumerate(rows):
            tile = jnp.where(iota((16, lanes), 0) == r, row, tile)
        target, rest, cot, _ = columns_of(tile)
        wanted_ref[...] = target
        small_ref[:tokens] = jnp.where(iota((tokens, lanes), 1) == 0, rest, cot)
        small_ref[tokens:] = jnp.zeros((shards * chunk - tokens, lanes), f32)
        h = jnp.transpose(h_ref[...])
        for i in range(4):
            at = pl.multiple_of(index_ref[0] * 1024 + i * 256, 256)
            part = jnp.dot(h, w_ref[:, pl.ds(at, 256)], preferred_element_type=f32)
            out_ref[2 * i] = part[:, :lanes]
            out_ref[2 * i + 1] = part[:, lanes:]

    out = [
        jax.ShapeDtypeStruct((8, tokens, lanes), f32),
        jax.ShapeDtypeStruct((tokens, lanes), f32),
        jax.ShapeDtypeStruct((shards * chunk, lanes), f32),
    ]
    return call(kernel, out, [smem] + [vmem] * 5)(index, hidden_t, weight_t, *vectors)


def add_halves(kept, received):
    def kernel(kept_ref, received_ref, out_ref):
        for i in range(8):
            out_ref[i] = (kept_ref[i] + received_ref[i].astype(f32)).astype(bf16)

    return call(kernel, jax.ShapeDtypeStruct(kept.shape, bf16), [vmem, vmem])(kept, received)


def high_low(tile):
    high = tile.astype(bf16).astype(f32)
    return [high, tile - high]


def soften(index, parts, target):
    def kernel(index_ref, parts_ref, target_ref, out_ref):
        logits = parts_ref[0].astype(f32)
        for i in range(1, 8):
            logits = logits + parts_ref[i].astype(f32)
        ratio = jnp.tanh(logits * (1.0 / soft_cap))
        capped = soft_cap * ratio
        power = jnp.exp(capped - soft_cap)
        soft = (power * (1.0 - ratio * ratio)).astype(bf16)
        first = index_ref[1] + index_ref[0] * 1024 + (index_ref[2] // 2) * lanes
        columns = (iota((1, lanes), 1) + first).astype(f32)
        hit = jnp.where(columns == target_ref[...], capped, 0.0)

        def total(block):
            return lax.dot_general(
                jnp.ones((8, lanes), f32),
                block,
                (((1,), (1,)), ((), ())),
                precision=lax.Precision.HIGHEST,
                preferred_element_type=f32,
            )[0:1]

        row = iota((16, lanes), 0)
        tile = jnp.zeros((16, lanes), f32)
        for k, sums in enumerate((total(power), total(hit))):
            for r, piece in enumerate(rows_of(sums)):
                high, low = high_low(piece)
                tile = jnp.where(row == 8 * k + r, high, tile)
                tile = jnp.where(row == 8 * k + 4 + r, low, tile)
        tile = tile.astype(bf16)
        out_ref[:filled] = soft.reshape(filled, chunk, lanes)
        out_ref[filled] = tile

    out = jax.ShapeDtypeStruct((filled + 1, chunk, lanes), bf16)
    return call(kernel, out, [smem, vmem, vmem])(index, parts, target)


def half_grad(index, soft, target, small, weight_t, before=()):
    depth = weight_t.shape[0]
    last = bool(before)

    def kernel(index_ref, soft_ref, target_ref, small_ref, w_ref, *refs):
        sums = jnp.zeros((chunk, lanes), f32)
        for i in range(8):
            sums = sums + soft_ref[filled, i].astype(f32)
        if last:
            sums = sums + refs[1][...]
        rows = [sums[0:4] + sums[4:8], sums[8:12] + sums[12:16]]
        power, picked = columns_of(jnp.concatenate(rows, axis=0))
        ratio = picked * (1.0 / soft_cap)
        cot = jnp.broadcast_to(small_ref[:tokens, 1:2], (tokens, lanes))
        hits = cot * (1.0 - ratio * ratio)
        total = refs[-1]
        which = 1 - index_ref[0] if last else index_ref[0]
        for j in range(4):
            at = pl.multiple_of(which * 1024 + j * 256, 256)
            blocks = []
            for k in range(2):
                column = (iota((1, lanes), 1) + (index_ref[1] + at + k * lanes)).astype(f32)
                hit = jnp.where(column == target_ref[...], hits, 0.0).astype(bf16)
                soft = soft_ref[:filled, 2 * j + k].reshape(tokens, lanes)
                blocks.append(jnp.concatenate([soft, hit], axis=0))
            product = lax.dot_general(
                jnp.concatenate(blocks, axis=1),
                w_ref[:, pl.ds(at, 256)],
                (((1,), (1,)), ((), ())),
                preferred_element_type=f32,
            )
            if j:
                total[...] += product
            elif last:
                total[...] = refs[0][...] + product
            else:
                total[...] = product
        if not last:
            refs[1][...] = sums
            return
        out_ref, hits_ref = refs[2:4]
        hits_ref[...] = hits
        first, second = total[:tokens], total[tokens:]
        lane = iota((tokens, lanes), 1)
        end = jnp.concatenate([second[:, 224:], jnp.zeros((tokens, lanes - depth + 224), f32)], axis=1)
        for k, column in enumerate(high_low(power) + high_low(picked)):
            end = jnp.where(lane == depth - 224 + k, column, end)
        middle = jnp.concatenate([first[:, 256:], second[:, :96]], axis=1)
        for t, piece in enumerate((first[:, :lanes], first[:, lanes:256], middle, second[:, 96:224], end)):
            out_ref[:filled, :, t * lanes : (t + 1) * lanes] = piece.astype(bf16).reshape(filled, chunk, lanes)
        out_ref[filled:] = jnp.zeros((shards - filled, chunk, packed), bf16)

    total = (2 * tokens, depth)
    if last:
        out = [
            jax.ShapeDtypeStruct((shards, chunk, packed), bf16),
            jax.ShapeDtypeStruct((tokens, lanes), f32),
        ]
        scratch = [pltpu.VMEM(total, f32)]
    else:
        out = [jax.ShapeDtypeStruct((chunk, lanes), f32), jax.ShapeDtypeStruct(total, f32)]
        out = [out[1], out[0]]
        scratch = []
    inside = kernel if last else lambda *refs: kernel(*refs, refs[5])
    return call(inside, out, [smem] + [vmem] * (4 + len(before)), scratch)(
        index, soft, target, small, weight_t, *before
    )


def reduce_chunk(index, parts, small, depth):
    def kernel(index_ref, parts_ref, small_ref, out_ref):
        total = parts_ref[0].astype(f32)
        for i in range(1, shards):
            total = total + parts_ref[i].astype(f32)
        mine = small_ref[pl.ds(pl.multiple_of(index_ref[3] * chunk, chunk), chunk)]
        rest, cot = mine[:, 0:1], mine[:, 1:2]
        at = 2 * depth
        power = total[:, at : at + 1] + total[:, at + 1 : at + 2]
        picked = total[:, at + 2 : at + 3] + total[:, at + 3 : at + 4]
        slab = jnp.log(power) + soft_cap
        larger, smaller = jnp.maximum(slab, rest), jnp.minimum(slab, rest)
        lse = larger + jnp.log(1.0 + jnp.exp(smaller - larger))
        loss = lse - picked + zloss_weight * lse * lse
        scale = cot * (1.0 + 2.0 * zloss_weight * lse) * jnp.exp(soft_cap - lse)
        out = total[:, :depth] * scale - total[:, depth:at]
        out = jnp.concatenate([out, jnp.zeros((chunk, padded - depth), f32)], axis=1)
        lane = iota((chunk, padded), 1)
        for k, column in enumerate(high_low(scale) + high_low(loss)):
            out = jnp.where(lane == depth + k, column, out)
        out = out.astype(bf16)
        for i in range(shards):
            out_ref[i] = out

    out = jax.ShapeDtypeStruct((shards, chunk, padded), bf16)
    return call(kernel, out, [smem, vmem, vmem])(index, parts, small)


def finish(index, reduced, own, other, hits, target, hidden_t):
    depth = hidden_t.shape[0]
    share = tokens // 16

    def kernel(
        index_ref, reduced_ref, own_ref, other_ref, hits_ref, target_ref, h_ref,
        gh_ref, gw_ref, loss_ref, scales, losses,
    ):
        last = reduced_ref[:filled, :, 256:].reshape(tokens, lanes).astype(f32)
        at = depth - 256
        scales[...] = jnp.broadcast_to(last[:, at : at + 1] + last[:, at + 1 : at + 2], (tokens, lanes))
        losses[:tokens] = jnp.broadcast_to(last[:, at + 2 : at + 3] + last[:, at + 3 : at + 4], (tokens, lanes))
        loss_ref[...] = jnp.transpose(losses[pl.ds(index_ref[2] * share, 32)])[0:1, :share]
        summed = reduced_ref[:filled].reshape(tokens, padded).astype(f32)
        gh_ref[...] = jnp.transpose(summed)[:depth].astype(bf16)
        for j in range(8):
            which = index_ref[0] if j < 4 else 1 - index_ref[0]
            at = pl.multiple_of(which * 1024 + (j % 4) * 256, 256)
            blocks = []
            for k in range(2):
                place = 2 * (j % 4) + k
                block = (own_ref if j < 4 else other_ref)[:filled, place].reshape(tokens, lanes)
                column = (iota((1, lanes), 1) + (index_ref[1] + at + k * lanes)).astype(f32)
                hit = jnp.where(column == target_ref[...], hits_ref[...], 0.0)
                blocks.append((block.astype(f32) * scales[...] - hit).astype(bf16))
            product = jnp.dot(
                h_ref[...], jnp.concatenate(blocks, axis=1), preferred_element_type=f32
            )
            gw_ref[:, pl.ds(at, 256)] = product.astype(bf16)

    return call(
        kernel,
        [
            jax.ShapeDtypeStruct((depth, tokens), bf16),
            jax.ShapeDtypeStruct((depth, 2048), bf16),
            jax.ShapeDtypeStruct((1, share), f32),
        ],
        [smem] + [vmem] * 6,
        [pltpu.VMEM((tokens, lanes), f32), pltpu.VMEM((tokens + 32, lanes), f32)],
    )(index, reduced, own, other, hits, target, hidden_t)


def per_device(hidden, head_weight, targets, lse_rest, cotangent):
    x, y, z, core = (lax.axis_index(a).astype(jnp.int32) for a in ("x", "y", "z", "core"))
    swap = [(0, 1), (1, 0)]
    vocab = ("x", "y")
    shard = x * 8 + y
    index = jnp.stack([core, shard * 2048, z * 2 + core, shard])
    hidden_t, weight_t = hidden.T, head_weight.T
    vectors = [v.reshape(1, tokens) for v in (targets, lse_rest, cotangent)]

    received = lax.ppermute(sent_logits(core.reshape(1), hidden_t, weight_t), "core", swap)
    kept, target, small = kept_logits(index, hidden_t, weight_t, vectors)
    parts = add_halves(kept, received)
    parts = lax.all_to_all(parts, "z", 0, 0, tiled=True)
    own = lax.all_gather(soften(index, parts, target), "z", axis=1)
    other = lax.ppermute(own, "core", swap)
    before = half_grad(index, own, target, small, weight_t)
    part, hits = half_grad(index, other, target, small, weight_t, before)
    shares = lax.all_to_all(part, vocab, 0, 0, tiled=True)
    spread = reduce_chunk(index, shares, small, hidden.shape[1])
    reduced = lax.all_to_all(spread, vocab, 0, 0, tiled=True)
    grad_hidden, grad_weight, token_loss = finish(
        index, reduced, own, other, hits, target, hidden_t
    )
    return (grad_hidden.T, grad_weight.T, token_loss.reshape(-1))


def solution(mesh):
    mesh = Mesh(mesh.devices.reshape(4, 8, 8, 2), ("x", "y", "z", "core"))
    vocab, width = ("x", "y"), ("z", "core")
    return jax.shard_map(
        per_device,
        mesh=mesh,
        in_specs=(P(None, width), P(vocab, width), P(), P(), P()),
        out_specs=(P(None, width), P(vocab, width), P(width)),
        check_vma=False,
    )
```

```python
import jax
import jax.numpy as jnp
from jax import lax
from jax.experimental import pallas as pl
from jax.experimental.pallas import tpu as pltpu
from jax.sharding import Mesh, PartitionSpec as P

soft_cap = 30.0
zloss_weight = 0.002
tokens = 448
lanes = 128
chunk = 16
shards = 32
filled = tokens // chunk
share = 14
tail_rows = 7
bf16, f32 = jnp.bfloat16, jnp.float32
vmem = pl.BlockSpec(memory_space=pltpu.VMEM)
smem = pl.BlockSpec(memory_space=pltpu.SMEM)
hbm = pl.BlockSpec(memory_space=pltpu.HBM)


def call(kernel, out_shape, in_specs, scratch=()):
    several = isinstance(out_shape, (list, tuple))
    return pl.pallas_call(
        kernel,
        in_specs=in_specs,
        out_specs=[vmem] * len(out_shape) if several else vmem,
        out_shape=out_shape,
        scratch_shapes=scratch,
        compiler_params=pltpu.CompilerParams(vmem_limit_bytes=32 * 1024 * 1024),
    )


def iota(shape, axis):
    return lax.broadcasted_iota(jnp.int32, shape, axis)


def rows_of(vector):
    out = [vector[:, r * lanes : (r + 1) * lanes] for r in range(3)]
    tail = jnp.zeros((1, 4 * lanes - tokens), vector.dtype)
    return out + [jnp.concatenate([vector[:, 3 * lanes :], tail], axis=1)]


def columns_of(rows):
    turned = jnp.transpose(rows)
    out = []
    for at in range(0, rows.shape[0], 4):
        pieces = [turned[: min(lanes, tokens - r * lanes), at + r : at + r + 1] for r in range(4)]
        out.append(jnp.broadcast_to(jnp.concatenate(pieces, axis=0), (tokens, lanes)))
    return out


def sent_logits(index, hidden_t, weight_t):
    depth = hidden_t.shape[0]

    def kernel(index_ref, h_hbm, w_hbm, out_ref, h_ref, w_ref, arrived):
        half = pl.multiple_of((1 - index_ref[0]) * 1024, 1024)
        first = pltpu.make_async_copy(h_hbm, h_ref, arrived.at[0])
        second = pltpu.make_async_copy(w_hbm.at[:, pl.ds(half, 1024)], w_ref, arrived.at[1])
        first.start()
        second.start()
        first.wait()
        h = jnp.transpose(h_ref[...])
        second.wait()
        for i in range(4):
            part = jnp.dot(h, w_ref[:, i * 256 : (i + 1) * 256], preferred_element_type=f32)
            out_ref[2 * i] = part[:, :lanes].astype(bf16)
            out_ref[2 * i + 1] = part[:, lanes:].astype(bf16)

    return pl.pallas_call(
        kernel,
        in_specs=[smem, hbm, hbm],
        out_specs=vmem,
        out_shape=jax.ShapeDtypeStruct((8, tokens, lanes), bf16),
        scratch_shapes=[
            pltpu.VMEM((depth, tokens), bf16),
            pltpu.VMEM((depth, 1024), bf16),
            pltpu.SemaphoreType.DMA((2,)),
        ],
        compiler_params=pltpu.CompilerParams(vmem_limit_bytes=60 * 1024 * 1024),
    )(index, hidden_t, weight_t)


def kept_logits(index, hidden_t, weight_t, vectors):
    def kernel(index_ref, h_ref, w_ref, target_ref, rest_ref, cot_ref, out_ref, wanted_ref, small_ref):
        rows = rows_of(target_ref[...].astype(f32)) + rows_of(rest_ref[...]) + rows_of(cot_ref[...])
        tile = jnp.zeros((16, lanes), f32)
        for r, row in enumerate(rows):
            tile = jnp.where(iota((16, lanes), 0) == r, row, tile)
        target, rest, cot, _ = columns_of(tile)
        wanted_ref[...] = target
        small_ref[:tokens] = jnp.where(iota((tokens, lanes), 1) == 0, rest, cot)
        small_ref[tokens:] = jnp.zeros((shards * chunk - tokens, lanes), f32)
        h = jnp.transpose(h_ref[...])
        for i in range(4):
            at = pl.multiple_of(index_ref[0] * 1024 + i * 256, 256)
            part = jnp.dot(h, w_ref[:, pl.ds(at, 256)], preferred_element_type=f32)
            out_ref[2 * i] = part[:, :lanes]
            out_ref[2 * i + 1] = part[:, lanes:]

    out = [
        jax.ShapeDtypeStruct((8, tokens, lanes), f32),
        jax.ShapeDtypeStruct((tokens, lanes), f32),
        jax.ShapeDtypeStruct((shards * chunk, lanes), f32),
    ]
    return call(kernel, out, [smem] + [vmem] * 5)(index, hidden_t, weight_t, *vectors)


def add_halves(kept, received):
    def kernel(kept_ref, received_ref, out_ref):
        for i in range(8):
            out_ref[i] = (kept_ref[i] + received_ref[i].astype(f32)).astype(bf16)

    return call(kernel, jax.ShapeDtypeStruct(kept.shape, bf16), [vmem, vmem])(kept, received)


def places(axis):
    shape = (shards * chunk, 1) if axis == 0 else (1, shards * chunk)
    row = iota(shape, axis)
    number, inside = row // chunk, row % chunk
    token = jnp.where(inside < share, number * share + inside, -1)
    group = jnp.where(inside < share, -1, number * 2 + inside - share)
    return token, group


def ones_where(condition):
    return jnp.where(condition, 1.0, 0.0).astype(bf16)


def exact(a, b):
    wide = a.dtype == f32 or b.dtype == f32
    precision = lax.Precision.HIGHEST if wide else None
    return jnp.dot(a, b, precision=precision, preferred_element_type=f32)


def repeated(tail, width, lanes_out, member):
    lane = iota((lanes, lanes_out), 1)
    spread = (lane % width == iota((lanes, lanes_out), 0)) & (lane < width * tail_rows)
    slot = iota((1, lanes_out), 1) // width
    return jnp.where(slot == member, exact(tail, ones_where(spread)), 0.0).astype(bf16)


def folded(wide, width, member):
    lanes_in = wide.shape[1]
    lane = iota((lanes_in, lanes), 0)
    fold = (lane % width == iota((lanes_in, lanes), 1)) & (lane < width * tail_rows)
    slot = iota((1, lanes_in), 1) // width
    mine = jnp.where(slot == member, wide, 0.0)
    fold = jnp.where(fold, 1.0, 0.0)
    return exact(mine, fold) if mine.dtype == f32 else exact(mine, fold.astype(bf16))


def high_low(tile):
    high = tile.astype(bf16).astype(f32)
    return [high, tile - high]


def soften(index, parts, target):
    def kernel(index_ref, parts_ref, target_ref, out_ref):
        logits = parts_ref[0].astype(f32)
        for i in range(1, 8):
            logits = logits + parts_ref[i].astype(f32)
        ratio = jnp.tanh(logits * (1.0 / soft_cap))
        capped = soft_cap * ratio
        power = jnp.exp(capped - soft_cap)
        soft = (power * (1.0 - ratio * ratio)).astype(bf16)
        first = index_ref[1] + index_ref[0] * 1024 + (index_ref[2] // 2) * lanes
        columns = (iota((1, lanes), 1) + first).astype(f32)
        hit = jnp.where(columns == target_ref[...], capped, 0.0)

        def total(block):
            return lax.dot_general(
                jnp.ones((8, lanes), f32),
                block,
                (((1,), (1,)), ((), ())),
                precision=lax.Precision.HIGHEST,
                preferred_element_type=f32,
            )[0:1]

        row = iota((16, lanes), 0)
        tile = jnp.zeros((16, lanes), f32)
        for k, sums in enumerate((total(power), total(hit))):
            for r, piece in enumerate(rows_of(sums)):
                high, low = high_low(piece)
                tile = jnp.where(row == 8 * k + r, high, tile)
                tile = jnp.where(row == 8 * k + 4 + r, low, tile)
        tile = tile.astype(bf16)
        out_ref[:filled] = soft.reshape(filled, chunk, lanes)
        out_ref[filled] = tile

    out = jax.ShapeDtypeStruct((filled + 1, chunk, lanes), bf16)
    return call(kernel, out, [smem, vmem, vmem])(index, parts, target)


def half_grad(index, soft, target, small, weight_t, before=()):
    depth = weight_t.shape[0]
    last = bool(before)

    def kernel(index_ref, soft_ref, target_ref, small_ref, w_ref, *refs):
        sums = jnp.zeros((chunk, lanes), f32)
        for i in range(8):
            sums = sums + soft_ref[filled, i].astype(f32)
        if last:
            sums = sums + refs[1][...]
        rows = [sums[0:4] + sums[4:8], sums[8:12] + sums[12:16]]
        power, picked = columns_of(jnp.concatenate(rows, axis=0))
        ratio = picked * (1.0 / soft_cap)
        cot = jnp.broadcast_to(small_ref[:tokens, 1:2], (tokens, lanes))
        hits = cot * (1.0 - ratio * ratio)
        total = refs[-1]
        which = 1 - index_ref[0] if last else index_ref[0]
        for j in range(4):
            at = pl.multiple_of(which * 1024 + j * 256, 256)
            blocks = []
            for k in range(2):
                column = (iota((1, lanes), 1) + (index_ref[1] + at + k * lanes)).astype(f32)
                hit = jnp.where(column == target_ref[...], hits, 0.0).astype(bf16)
                soft = soft_ref[:filled, 2 * j + k].reshape(tokens, lanes)
                blocks.append(jnp.concatenate([soft, hit], axis=0))
            product = lax.dot_general(
                jnp.concatenate(blocks, axis=1),
                w_ref[:, pl.ds(at, 256)],
                (((1,), (1,)), ((), ())),
                preferred_element_type=f32,
            )
            if j:
                total[...] += product
            elif last:
                total[...] = refs[0][...] + product
            else:
                total[...] = product
        if not last:
            refs[1][...] = sums
            return
        out_ref, hits_ref = refs[2:4]
        hits_ref[...] = hits
        first, second = total[:tokens], total[tokens:]
        lane = iota((tokens, lanes), 1)
        tail = jnp.concatenate([second[:, 224:], jnp.zeros((tokens, lanes - depth + 224), f32)], axis=1)
        for k, column in enumerate(high_low(power) + high_low(picked)):
            tail = jnp.where(lane == depth - 224 + k, column, tail)
        tail = repeated(tail.astype(bf16), depth - 220, 512, iota((tokens, 1), 0) % tail_rows)
        main = jnp.concatenate([first, second[:, :224]], axis=1).astype(bf16)
        token, group = places(0)
        each = iota((1, tokens), 1)
        choose = [ones_where(token == each), ones_where(group == each // tail_rows)]
        out = exact(jnp.concatenate(choose, axis=1), jnp.concatenate([main, tail], axis=0))
        out_ref[...] = out.astype(bf16).reshape(shards, chunk, 512)

    total = (2 * tokens, depth)
    if last:
        out = [
            jax.ShapeDtypeStruct((shards, chunk, 512), bf16),
            jax.ShapeDtypeStruct((tokens, lanes), f32),
        ]
        scratch = [pltpu.VMEM(total, f32)]
    else:
        out = [jax.ShapeDtypeStruct((chunk, lanes), f32), jax.ShapeDtypeStruct(total, f32)]
        out = [out[1], out[0]]
        scratch = []
    inside = kernel if last else lambda *refs: kernel(*refs, refs[5])
    return call(inside, out, [smem] + [vmem] * (4 + len(before)), scratch)(
        index, soft, target, small, weight_t, *before
    )


def reduce_chunk(index, parts, small, depth):
    def kernel(index_ref, parts_ref, small_ref, out_ref):
        total = parts_ref[0].astype(f32)
        for i in range(1, shards):
            total = total + parts_ref[i].astype(f32)
        mine = small_ref[pl.ds(index_ref[3] * share, chunk)]
        rest, cot = mine[:, 0:1], mine[:, 1:2]
        row, column = iota((chunk, 1), 0), iota((1, chunk), 1)
        own = (column == share + row // tail_rows) & (row < share)
        held = exact(jnp.where(own, 1.0, 0.0), total)
        tail = folded(held, depth - 220, row % tail_rows)
        at = depth - 224
        power = tail[:, at : at + 1] + tail[:, at + 1 : at + 2]
        picked = tail[:, at + 2 : at + 3] + tail[:, at + 3 : at + 4]
        slab = jnp.log(power) + soft_cap
        larger, smaller = jnp.maximum(slab, rest), jnp.minimum(slab, rest)
        lse = larger + jnp.log(1.0 + jnp.exp(smaller - larger))
        loss = lse - picked + zloss_weight * lse * lse
        scale = cot * (1.0 + 2.0 * zloss_weight * lse) * jnp.exp(soft_cap - lse)
        second = jnp.concatenate([total[:, depth:], tail[:, :at]], axis=1)
        out = jnp.where(row < share, total[:, :depth] * scale - second, 0.0)
        end = jnp.concatenate([out[:, 256:], jnp.zeros((chunk, lanes - depth + 256), f32)], axis=1)
        lane = iota((chunk, lanes), 1)
        for k, column_k in enumerate(high_low(scale) + high_low(loss)):
            end = jnp.where((lane == depth - 256 + k) & (row < share), column_k, end)
        end = repeated(end.astype(bf16), depth - 252, 256, row % tail_rows)
        into = ones_where((row == share + column // tail_rows) & (column < share))
        out = (out[:, :256] + exact(into, end)).astype(bf16)
        for i in range(shards):
            out_ref[i] = out

    out = jax.ShapeDtypeStruct((shards, chunk, 256), bf16)
    return call(kernel, out, [smem, vmem, vmem])(index, parts, small)


def finish(index, reduced, own, other, hits, target, hidden_t):
    depth = hidden_t.shape[0]
    losses_each = tokens // 16

    def kernel(
        index_ref, reduced_ref, own_ref, other_ref, hits_ref, target_ref, h_ref,
        gh_ref, gw_ref, loss_ref, scales, losses,
    ):
        token, group = places(1)
        each = iota((tokens, 1), 0)
        choose = [ones_where(token == each), ones_where(group == each // tail_rows)]
        held = exact(jnp.concatenate(choose, axis=0), reduced_ref[...].reshape(shards * chunk, 256))
        last = folded(held[tokens:].astype(bf16), depth - 252, each % tail_rows)
        at = depth - 256
        scales[...] = jnp.broadcast_to(last[:, at : at + 1] + last[:, at + 1 : at + 2], (tokens, lanes))
        losses[:tokens] = jnp.broadcast_to(last[:, at + 2 : at + 3] + last[:, at + 3 : at + 4], (tokens, lanes))
        loss_ref[...] = jnp.transpose(losses[pl.ds(index_ref[2] * losses_each, 32)])[0:1, :losses_each]
        gh_ref[:256] = jnp.transpose(held[:tokens]).astype(bf16)
        gh_ref[256:] = jnp.transpose(last)[:at].astype(bf16)
        for j in range(8):
            which = index_ref[0] if j < 4 else 1 - index_ref[0]
            at = pl.multiple_of(which * 1024 + (j % 4) * 256, 256)
            blocks = []
            for k in range(2):
                place = 2 * (j % 4) + k
                block = (own_ref if j < 4 else other_ref)[:filled, place].reshape(tokens, lanes)
                column = (iota((1, lanes), 1) + (index_ref[1] + at + k * lanes)).astype(f32)
                hit = jnp.where(column == target_ref[...], hits_ref[...], 0.0)
                blocks.append((block.astype(f32) * scales[...] - hit).astype(bf16))
            product = jnp.dot(
                h_ref[...], jnp.concatenate(blocks, axis=1), preferred_element_type=f32
            )
            gw_ref[:, pl.ds(at, 256)] = product.astype(bf16)

    return call(
        kernel,
        [
            jax.ShapeDtypeStruct((depth, tokens), bf16),
            jax.ShapeDtypeStruct((depth, 2048), bf16),
            jax.ShapeDtypeStruct((1, losses_each), f32),
        ],
        [smem] + [vmem] * 6,
        [pltpu.VMEM((tokens, lanes), f32), pltpu.VMEM((tokens + 32, lanes), f32)],
    )(index, reduced, own, other, hits, target, hidden_t)


def per_device(hidden, head_weight, targets, lse_rest, cotangent):
    x, y, z, core = (lax.axis_index(a).astype(jnp.int32) for a in ("x", "y", "z", "core"))
    swap = [(0, 1), (1, 0)]
    vocab = ("x", "y")
    shard = x * 8 + y
    index = jnp.stack([core, shard * 2048, z * 2 + core, shard])
    hidden_t, weight_t = hidden.T, head_weight.T
    vectors = [v.reshape(1, tokens) for v in (targets, lse_rest, cotangent)]

    received = lax.ppermute(sent_logits(core.reshape(1), hidden_t, weight_t), "core", swap)
    kept, target, small = kept_logits(index, hidden_t, weight_t, vectors)
    parts = add_halves(kept, received)
    parts = lax.all_to_all(parts, "z", 0, 0, tiled=True)
    own = lax.all_gather(soften(index, parts, target), "z", axis=1)
    other = lax.ppermute(own, "core", swap)
    before = half_grad(index, own, target, small, weight_t)
    part, hits = half_grad(index, other, target, small, weight_t, before)
    shares = lax.all_to_all(part, vocab, 0, 0, tiled=True)
    spread = reduce_chunk(index, shares, small, hidden.shape[1])
    reduced = lax.all_to_all(spread, vocab, 0, 0, tiled=True)
    grad_hidden, grad_weight, token_loss = finish(
        index, reduced, own, other, hits, target, hidden_t
    )
    return (grad_hidden.T, grad_weight.T, token_loss.reshape(-1))


def solution(mesh):
    mesh = Mesh(mesh.devices.reshape(4, 8, 8, 2), ("x", "y", "z", "core"))
    vocab, width = ("x", "y"), ("z", "core")
    return jax.shard_map(
        per_device,
        mesh=mesh,
        in_specs=(P(None, width), P(vocab, width), P(), P(), P()),
        out_specs=(P(None, width), P(vocab, width), P(width)),
        check_vma=False,
    )
```

```python
import jax
import jax.numpy as jnp
from jax import lax
from jax.experimental import pallas as pl
from jax.experimental.pallas import tpu as pltpu
from jax.sharding import Mesh, PartitionSpec as P

soft_cap = 30.0
zloss_weight = 0.002
tokens = 448
lanes = 128
chunk = 16
shards = 32
filled = tokens // chunk
share = 14
tail_rows = 7
bf16, f32 = jnp.bfloat16, jnp.float32
vmem = pl.BlockSpec(memory_space=pltpu.VMEM)
smem = pl.BlockSpec(memory_space=pltpu.SMEM)
hbm = pl.BlockSpec(memory_space=pltpu.HBM)


def call(kernel, out_shape, in_specs, scratch=()):
    several = isinstance(out_shape, (list, tuple))
    return pl.pallas_call(
        kernel,
        in_specs=in_specs,
        out_specs=[vmem] * len(out_shape) if several else vmem,
        out_shape=out_shape,
        scratch_shapes=scratch,
        compiler_params=pltpu.CompilerParams(vmem_limit_bytes=32 * 1024 * 1024),
    )


def iota(shape, axis):
    return lax.broadcasted_iota(jnp.int32, shape, axis)


def rows_of(vector):
    out = [vector[:, r * lanes : (r + 1) * lanes] for r in range(3)]
    tail = jnp.zeros((1, 4 * lanes - tokens), vector.dtype)
    return out + [jnp.concatenate([vector[:, 3 * lanes :], tail], axis=1)]


def columns_of(rows):
    turned = jnp.transpose(rows)
    out = []
    for at in range(0, rows.shape[0], 4):
        pieces = [turned[: min(lanes, tokens - r * lanes), at + r : at + r + 1] for r in range(4)]
        out.append(jnp.broadcast_to(jnp.concatenate(pieces, axis=0), (tokens, lanes)))
    return out


def sent_logits(index, hidden_t, weight_t):
    depth = hidden_t.shape[0]

    def kernel(index_ref, h_hbm, w_hbm, out_ref, h_ref, w_ref, arrived):
        half = pl.multiple_of((1 - index_ref[0]) * 1024, 1024)
        first = pltpu.make_async_copy(h_hbm, h_ref, arrived.at[0])
        second = pltpu.make_async_copy(w_hbm.at[:, pl.ds(half, 1024)], w_ref, arrived.at[1])
        first.start()
        second.start()
        first.wait()
        h = jnp.transpose(h_ref[...])
        second.wait()
        for i in range(4):
            part = jnp.dot(h, w_ref[:, i * 256 : (i + 1) * 256], preferred_element_type=f32)
            out_ref[2 * i] = part[:, :lanes].astype(bf16)
            out_ref[2 * i + 1] = part[:, lanes:].astype(bf16)

    return pl.pallas_call(
        kernel,
        in_specs=[smem, hbm, hbm],
        out_specs=vmem,
        out_shape=jax.ShapeDtypeStruct((8, tokens, lanes), bf16),
        scratch_shapes=[
            pltpu.VMEM((depth, tokens), bf16),
            pltpu.VMEM((depth, 1024), bf16),
            pltpu.SemaphoreType.DMA((2,)),
        ],
        compiler_params=pltpu.CompilerParams(vmem_limit_bytes=60 * 1024 * 1024),
    )(index, hidden_t, weight_t)


def kept_logits(index, hidden_t, weight_t, vectors):
    def kernel(
        index_ref, h_ref, w_ref, target_ref, rest_ref, cot_ref,
        out_ref, wanted_ref, small_ref, pack_ref, unpack_ref,
    ):
        rows = rows_of(target_ref[...].astype(f32)) + rows_of(rest_ref[...]) + rows_of(cot_ref[...])
        tile = jnp.zeros((16, lanes), f32)
        for r, row in enumerate(rows):
            tile = jnp.where(iota((16, lanes), 0) == r, row, tile)
        target, rest, cot, _ = columns_of(tile)
        wanted_ref[...] = target
        small_ref[:tokens] = jnp.where(iota((tokens, lanes), 1) == 0, rest, cot)
        small_ref[tokens:] = jnp.zeros((shards * chunk - tokens, lanes), f32)
        h = jnp.transpose(h_ref[...])
        for i in range(4):
            at = pl.multiple_of(index_ref[0] * 1024 + i * 256, 256)
            part = jnp.dot(h, w_ref[:, pl.ds(at, 256)], preferred_element_type=f32)
            out_ref[2 * i] = part[:, :lanes]
            out_ref[2 * i + 1] = part[:, lanes:]
        for axis, ref in enumerate((pack_ref, unpack_ref)):
            token, group = places(axis)
            each = iota((tokens, 1) if axis else (1, tokens), 1 - axis)
            choose = [ones_where(token == each.astype(f32)), ones_where(group == divided(each, tail_rows)[0])]
            ref[...] = jnp.concatenate(choose, axis=1 - axis)

    out = [
        jax.ShapeDtypeStruct((8, tokens, lanes), f32),
        jax.ShapeDtypeStruct((tokens, lanes), f32),
        jax.ShapeDtypeStruct((shards * chunk, lanes), f32),
        jax.ShapeDtypeStruct((shards * chunk, 2 * tokens), bf16),
        jax.ShapeDtypeStruct((2 * tokens, shards * chunk), bf16),
    ]
    return call(kernel, out, [smem] + [vmem] * 5)(index, hidden_t, weight_t, *vectors)


def add_halves(kept, received):
    def kernel(kept_ref, received_ref, out_ref):
        for i in range(8):
            out_ref[i] = (kept_ref[i] + received_ref[i].astype(f32)).astype(bf16)

    return call(kernel, jax.ShapeDtypeStruct(kept.shape, bf16), [vmem, vmem])(kept, received)


def divided(count, by):
    count = count.astype(f32)
    quotient = jnp.floor((count + 0.5) * (1.0 / by))
    return quotient, count - quotient * by


def places(axis):
    shape = (shards * chunk, 1) if axis == 0 else (1, shards * chunk)
    number, inside = divided(iota(shape, axis), chunk)
    token = jnp.where(inside < share, number * share + inside, -1.0)
    group = jnp.where(inside < share, -1.0, number * 2 + inside - share)
    return token, group


def ones_where(condition):
    return jnp.where(condition, 1.0, 0.0).astype(bf16)


def exact(a, b):
    return jnp.dot(a, b, preferred_element_type=f32)


def repeated(tail, width, lanes_out, member):
    slot, place = divided(iota((1, lanes_out), 1), width)
    spread = jnp.where(slot < tail_rows, place, -1.0) == iota((lanes, lanes_out), 0).astype(f32)
    return jnp.where(slot == member, exact(tail, ones_where(spread)), 0.0).astype(bf16)


def folded(wide, width, member):
    lanes_in = wide.shape[1]
    slot, place = divided(iota((lanes_in, 1), 0), width)
    fold = jnp.where(slot < tail_rows, place, -1.0) == iota((1, lanes), 1).astype(f32)
    slot = divided(iota((1, lanes_in), 1), width)[0]
    mine = jnp.where(slot == member, wide, 0.0)
    return exact(mine, ones_where(fold))


def high_low(tile):
    high = tile.astype(bf16).astype(f32)
    return [high, tile - high]


def soften(index, parts, target):
    def kernel(index_ref, parts_ref, target_ref, out_ref):
        logits = parts_ref[0].astype(f32)
        for i in range(1, 8):
            logits = logits + parts_ref[i].astype(f32)
        ratio = jnp.tanh(logits * (1.0 / soft_cap))
        capped = soft_cap * ratio
        power = jnp.exp(capped - soft_cap)
        soft = (power * (1.0 - ratio * ratio)).astype(bf16)
        first = index_ref[1] + index_ref[0] * 1024 + (index_ref[2] // 2) * lanes
        columns = (iota((1, lanes), 1) + first).astype(f32)
        hit = jnp.where(columns == target_ref[...], capped, 0.0)

        def total(block):
            return lax.dot_general(
                jnp.ones((16, 2 * lanes), bf16),
                jnp.concatenate([part.astype(bf16) for part in high_low(block)], axis=1),
                (((1,), (1,)), ((), ())),
                preferred_element_type=f32,
            )[0:1]

        row = iota((16, lanes), 0)
        tile = jnp.zeros((16, lanes), f32)
        for k, sums in enumerate((total(power), total(hit))):
            for r, piece in enumerate(rows_of(sums)):
                high, low = high_low(piece)
                tile = jnp.where(row == 8 * k + r, high, tile)
                tile = jnp.where(row == 8 * k + 4 + r, low, tile)
        tile = tile.astype(bf16)
        out_ref[:filled] = soft.reshape(filled, chunk, lanes)
        out_ref[filled] = tile

    out = jax.ShapeDtypeStruct((filled + 1, chunk, lanes), bf16)
    return call(kernel, out, [smem, vmem, vmem])(index, parts, target)


def half_grad(index, soft, target, small, weight_t, before=()):
    depth = weight_t.shape[0]
    last = bool(before)

    def kernel(index_ref, soft_ref, target_ref, small_ref, w_ref, *refs):
        sums = jnp.zeros((chunk, lanes), f32)
        for i in range(8):
            sums = sums + soft_ref[filled, i].astype(f32)
        if last:
            sums = sums + refs[1][...]
        rows = [sums[0:4] + sums[4:8], sums[8:12] + sums[12:16]]
        power, picked = columns_of(jnp.concatenate(rows, axis=0))
        ratio = picked * (1.0 / soft_cap)
        cot = jnp.broadcast_to(small_ref[:tokens, 1:2], (tokens, lanes))
        hits = cot * (1.0 - ratio * ratio)
        total = refs[-1]
        which = 1 - index_ref[0] if last else index_ref[0]
        for j in range(4):
            at = pl.multiple_of(which * 1024 + j * 256, 256)
            blocks = []
            for k in range(2):
                column = (iota((1, lanes), 1) + (index_ref[1] + at + k * lanes)).astype(f32)
                hit = jnp.where(column == target_ref[...], hits, 0.0).astype(bf16)
                soft = soft_ref[:filled, 2 * j + k].reshape(tokens, lanes)
                blocks.append(jnp.concatenate([soft, hit], axis=0))
            product = lax.dot_general(
                jnp.concatenate(blocks, axis=1),
                w_ref[:, pl.ds(at, 256)],
                (((1,), (1,)), ((), ())),
                preferred_element_type=f32,
            )
            if j:
                total[...] += product
            elif last:
                total[...] = refs[0][...] + product
            else:
                total[...] = product
        if not last:
            refs[1][...] = sums
            return
        pack_ref, out_ref, hits_ref = refs[2:5]
        hits_ref[...] = hits
        first, second = total[:tokens], total[tokens:]
        lane = iota((tokens, lanes), 1)
        tail = jnp.concatenate([second[:, 224:], jnp.zeros((tokens, lanes - depth + 224), f32)], axis=1)
        for k, column in enumerate(high_low(power) + high_low(picked)):
            tail = jnp.where(lane == depth - 224 + k, column, tail)
        tail = repeated(tail.astype(bf16), depth - 220, 512, divided(iota((tokens, 1), 0), tail_rows)[1])
        main = jnp.concatenate([first, second[:, :224]], axis=1).astype(bf16)
        out = exact(pack_ref[...], jnp.concatenate([main, tail], axis=0))
        out_ref[...] = out.astype(bf16).reshape(shards, chunk, 512)

    total = (2 * tokens, depth)
    if last:
        out = [
            jax.ShapeDtypeStruct((shards, chunk, 512), bf16),
            jax.ShapeDtypeStruct((tokens, lanes), f32),
        ]
        scratch = [pltpu.VMEM(total, f32)]
    else:
        out = [jax.ShapeDtypeStruct((chunk, lanes), f32), jax.ShapeDtypeStruct(total, f32)]
        out = [out[1], out[0]]
        scratch = []
    inside = kernel if last else lambda *refs: kernel(*refs, refs[5])
    return call(inside, out, [smem] + [vmem] * (4 + len(before)), scratch)(
        index, soft, target, small, weight_t, *before
    )


def reduce_chunk(index, parts, small, depth):
    def kernel(index_ref, parts_ref, small_ref, out_ref):
        total = parts_ref[0].astype(f32)
        for i in range(1, shards):
            total = total + parts_ref[i].astype(f32)
        mine = small_ref[pl.ds(index_ref[3] * share, chunk)]
        rest, cot = mine[:, 0:1], mine[:, 1:2]
        row = iota((chunk, 1), 0)
        group, member = divided(row, tail_rows)
        held = jnp.where(row < tail_rows, total[share : share + 1], total[share + 1 : share + 2])
        width = depth - 220
        tail = jnp.zeros((chunk, width), f32)
        for k in range(tail_rows):
            tail = jnp.where(member == k, held[:, k * width : (k + 1) * width], tail)
        at = depth - 224
        power = tail[:, at : at + 1] + tail[:, at + 1 : at + 2]
        picked = tail[:, at + 2 : at + 3] + tail[:, at + 3 : at + 4]
        slab = jnp.log(power) + soft_cap
        larger, smaller = jnp.maximum(slab, rest), jnp.minimum(slab, rest)
        lse = larger + jnp.log(1.0 + jnp.exp(smaller - larger))
        loss = lse - picked + zloss_weight * lse * lse
        scale = cot * (1.0 + 2.0 * zloss_weight * lse) * jnp.exp(soft_cap - lse)
        second = jnp.concatenate([total[:, depth:], tail[:, :at]], axis=1)
        out = jnp.where(row < share, total[:, :depth] * scale - second, 0.0)
        end = jnp.concatenate([out[:, 256:], jnp.zeros((chunk, lanes - depth + 256), f32)], axis=1)
        lane = iota((chunk, lanes), 1)
        for k, column_k in enumerate(high_low(scale) + high_low(loss)):
            end = jnp.where((lane == depth - 256 + k) & (row < share), column_k, end)
        end = repeated(end.astype(bf16), depth - 252, 256, member).astype(f32)
        out = out[:, :256]
        for k in range(2):
            ends = jnp.sum(jnp.where(group == k, end, 0.0), axis=0, keepdims=True)
            out = jnp.where(row == share + k, ends, out)
        out = out.astype(bf16)
        for i in range(shards):
            out_ref[i] = out

    out = jax.ShapeDtypeStruct((shards, chunk, 256), bf16)
    return call(kernel, out, [smem, vmem, vmem])(index, parts, small)


def finish(index, reduced, own, other, hits, target, unpack, hidden_t):
    depth = hidden_t.shape[0]
    losses_each = tokens // 16

    def kernel(
        index_ref, reduced_ref, own_ref, other_ref, hits_ref, target_ref, unpack_ref, h_ref,
        gh_ref, gw_ref, loss_ref, scales, losses,
    ):
        held = exact(unpack_ref[...], reduced_ref[...].reshape(shards * chunk, 256))
        last = folded(held[tokens:].astype(bf16), depth - 252, divided(iota((tokens, 1), 0), tail_rows)[1])
        at = depth - 256
        scales[...] = jnp.broadcast_to(last[:, at : at + 1] + last[:, at + 1 : at + 2], (tokens, lanes))
        losses[:tokens] = jnp.broadcast_to(last[:, at + 2 : at + 3] + last[:, at + 3 : at + 4], (tokens, lanes))
        loss_ref[...] = jnp.transpose(losses[pl.ds(index_ref[2] * losses_each, 32)])[0:1, :losses_each]
        gh_ref[:256] = jnp.transpose(held[:tokens]).astype(bf16)
        gh_ref[256:] = jnp.transpose(last)[:at].astype(bf16)
        for j in range(8):
            which = index_ref[0] if j < 4 else 1 - index_ref[0]
            at = pl.multiple_of(which * 1024 + (j % 4) * 256, 256)
            blocks = []
            for k in range(2):
                place = 2 * (j % 4) + k
                block = (own_ref if j < 4 else other_ref)[:filled, place].reshape(tokens, lanes)
                column = (iota((1, lanes), 1) + (index_ref[1] + at + k * lanes)).astype(f32)
                hit = jnp.where(column == target_ref[...], hits_ref[...], 0.0)
                blocks.append((block.astype(f32) * scales[...] - hit).astype(bf16))
            product = jnp.dot(
                h_ref[...], jnp.concatenate(blocks, axis=1), preferred_element_type=f32
            )
            gw_ref[:, pl.ds(at, 256)] = product.astype(bf16)

    return call(
        kernel,
        [
            jax.ShapeDtypeStruct((depth, tokens), bf16),
            jax.ShapeDtypeStruct((depth, 2048), bf16),
            jax.ShapeDtypeStruct((1, losses_each), f32),
        ],
        [smem] + [vmem] * 7,
        [pltpu.VMEM((tokens, lanes), f32), pltpu.VMEM((tokens + 32, lanes), f32)],
    )(index, reduced, own, other, hits, target, unpack, hidden_t)


def per_device(hidden, head_weight, targets, lse_rest, cotangent):
    x, y, z, core = (lax.axis_index(a).astype(jnp.int32) for a in ("x", "y", "z", "core"))
    swap = [(0, 1), (1, 0)]
    vocab = ("x", "y")
    shard = x * 8 + y
    index = jnp.stack([core, shard * 2048, z * 2 + core, shard])
    hidden_t, weight_t = hidden.T, head_weight.T
    vectors = [v.reshape(1, tokens) for v in (targets, lse_rest, cotangent)]

    received = lax.ppermute(sent_logits(core.reshape(1), hidden_t, weight_t), "core", swap)
    kept, target, small, pack, unpack = kept_logits(index, hidden_t, weight_t, vectors)
    parts = add_halves(kept, received)
    parts = lax.all_to_all(parts, "z", 0, 0, tiled=True)
    own = lax.all_gather(soften(index, parts, target), "z", axis=1)
    other = lax.ppermute(own, "core", swap)
    before = half_grad(index, own, target, small, weight_t)
    part, hits = half_grad(index, other, target, small, weight_t, (*before, pack))
    shares = lax.all_to_all(part, vocab, 0, 0, tiled=True)
    spread = reduce_chunk(index, shares, small, hidden.shape[1])
    reduced = lax.all_to_all(spread, vocab, 0, 0, tiled=True)
    grad_hidden, grad_weight, token_loss = finish(
        index, reduced, own, other, hits, target, unpack, hidden_t
    )
    return (grad_hidden.T, grad_weight.T, token_loss.reshape(-1))


def solution(mesh):
    mesh = Mesh(mesh.devices.reshape(4, 8, 8, 2), ("x", "y", "z", "core"))
    vocab, width = ("x", "y"), ("z", "core")
    return jax.shard_map(
        per_device,
        mesh=mesh,
        in_specs=(P(None, width), P(vocab, width), P(), P(), P()),
        out_specs=(P(None, width), P(vocab, width), P(width)),
        check_vma=False,
    )
```
